32 devices in a mesh: gy: 8 (over y, x, core), gx: 4 (over z).
Axes of the slice: x: 2, y: 2, z: 4, core: 2. Of those that a mesh axis runs over, the one named last changes fastest.
Arguments:
- even_half: float32 [32, 128, 1024], P('gx', None, 'gy'), may hold values from -90 to 90
- odd_half: float32 [32, 128, 1024], P('gx', None, 'gy'), may hold values from -90 to 90
- slab_slices: int32 [32], replicated, may hold values from 0 to 31, each once
- shells: int32 [32, 32, 32], replicated, may hold values from 0 to 16, as said below
Outputs:
- filtered: float32 [32, 128, 1024], P(None, 'gy', 'gx')
The draws below stay inside these ranges and needn't reach their ends.
Inputs may be any that keep to these rules, and one draw needn't show every extreme that they name: `slab_slices`: each slot holds a different z slice. `shells`: the zero frequency is in shell 0 and every shell number occurs.
All inputs are finite; a program needn't handle non-finite values.
Results may differ from the reference program's by a relative error of at most 0.0003.
Values sent between devices are 32-bit elements; how exact they have to be, the bound alone decides.
A program may use at most 192 MiB of HBM per device.

```python
import math
import jax
import jax.numpy as jnp
from jax import lax

Z = 32
BOX = 32
SHELLS = 17
Y = 128
X = 1024


def smooth_axis(field, axis):
    outer = jnp.roll(field, 2, axis) + jnp.roll(field, -2, axis)
    inner = jnp.roll(field, 1, axis) + jnp.roll(field, -1, axis)
    return (outer + 4.0 * inner + 6.0 * field) * (1.0 / 16.0)


def common_signal(key):
    base = jax.random.fold_in(key, 101)
    first, second = jax.random.split(base, 2)
    amp_grid = jnp.exp(jax.random.uniform(first, (Y // 32, X // 32), jnp.float32, math.log(0.3), math.log(20.0)))
    amplitude = jnp.repeat(jnp.repeat(amp_grid, 32, axis=0), 32, axis=1)
    rough = jax.random.truncated_normal(second, -4.0, 4.0, (Z, Y, X), jnp.float32)
    field = rough * amplitude
    field = smooth_axis(field, 0)
    field = smooth_axis(field, 1)
    field = smooth_axis(field, 2)
    return field


def noisy_half(key, salt):
    signal = common_signal(key)
    noise_key = jax.random.fold_in(key, salt)
    noise = 0.3 * jax.random.truncated_normal(noise_key, -4.0, 4.0, (Z, Y, X), jnp.float32)
    return signal + noise


def draw_even_half(key, part):
    return noisy_half(key, 202)


def draw_odd_half(key, part):
    return noisy_half(key, 303)


def draw_shells(key, part):
    freq = jnp.arange(BOX, dtype=jnp.int32)
    freq = jnp.where(freq < BOX // 2, freq, freq - BOX)
    radius_sq = freq[:, None, None] ** 2 + freq[None, :, None] ** 2 + freq[None, None, :] ** 2
    jitter = jax.random.randint(key, (BOX, BOX, BOX), -6, 7, jnp.int32)
    levels = jnp.arange(1, SHELLS, dtype=jnp.int32)
    counted = jnp.sum(((levels * levels)[:, None, None, None] <= (radius_sq + jitter)[None]).astype(jnp.int32), axis=0)
    return jnp.where(radius_sq == 0, 0, counted).astype(jnp.int32)


def setup_inputs(seed: int = 0) -> dict:
    seeds = jax.random.split(jax.random.key(seed), 5)
    return {
        "even_half": draw_even_half(jax.random.fold_in(seeds[4], 71), 0),
        "odd_half": draw_odd_half(jax.random.fold_in(seeds[4], 71), 0),
        "slab_slices": jax.random.permutation(seeds[2], Z).astype(jnp.int32),
        "shells": draw_shells(jax.random.fold_in(seeds[4], 71), 0),
    }


def make_tables():
    indices = jnp.arange(32, dtype=jnp.int32)
    angles = 2.0 * math.pi / 32.0 * (indices[:, None] * indices[None, :] % 32).astype(jnp.float32)
    cosines = jnp.cos(angles)
    sine_table = jnp.sin(angles)
    fwd_real = jnp.stack([cosines, -sine_table])
    fwd_cplx = jnp.stack([jnp.stack([cosines, sine_table], axis=1), jnp.stack([-sine_table, cosines], axis=1)])
    inv_cplx = jnp.stack([jnp.stack([cosines, -sine_table], axis=1), jnp.stack([sine_table, cosines], axis=1)])
    inv_real = jnp.stack([cosines, -sine_table], axis=1)
    taper_window = jnp.sin(math.pi * (indices.astype(jnp.float32) + 0.5) / 32.0)
    return (fwd_real, fwd_cplx, inv_cplx, inv_real, taper_window)

def filter_strip(strip, onehot, tables, col_weight):
    fwd_real, fwd_cplx, inv_cplx, inv_real, taper_window = tables
    halves, depth, height, width_x = strip.shape
    box_cols = width_x // 16 - 1
    blocks = strip.reshape(halves, depth, height, box_cols + 1, 16)
    box_stack = jnp.concatenate([blocks[:, :, :, :-1], blocks[:, :, :, 1:]], axis=4)
    box_stack = box_stack * taper_window[:, None, None] * taper_window * col_weight[:, None]
    highest = lax.Precision.HIGHEST
    spectra = jnp.einsum('pkn,hzybn->hpzykb', fwd_real, box_stack, precision=highest)
    spectra = jnp.einsum('qkpn,hpznxb->hqzkxb', fwd_cplx, spectra, precision=highest)
    spectra = jnp.einsum('qkpn,hpnyxb->hqkyxb', fwd_cplx, spectra, precision=highest)
    spectra = spectra.reshape(halves, 2, depth * height * 32, box_cols)
    cross_power = spectra[0, 0] * spectra[1, 0] + spectra[0, 1] * spectra[1, 1]
    power_even = spectra[0, 0] * spectra[0, 0] + spectra[0, 1] * spectra[0, 1]
    power_odd = spectra[1, 0] * spectra[1, 0] + spectra[1, 1] * spectra[1, 1]
    shell_sums = jnp.einsum('sv,mvb->msb', onehot, jnp.stack([cross_power, power_even, power_odd]), precision=highest)
    correlation = shell_sums[0] / jnp.sqrt(shell_sums[1] * shell_sums[2] + 1e-06)
    positive = jnp.maximum(correlation, 0.0)
    weights = 2.0 * positive / (1.0 + positive)
    voxel_weight = jnp.einsum('sv,sb->vb', onehot, weights, precision=highest)
    averaged = (spectra[0] + spectra[1]) * 0.5 * voxel_weight
    averaged = averaged.reshape(2, depth, height, 32, box_cols)
    averaged = jnp.einsum('qnpk,pkyxb->qnyxb', inv_cplx, averaged, precision=highest)
    averaged = jnp.einsum('qnpk,pzkxb->qznxb', inv_cplx, averaged, precision=highest)
    result = jnp.einsum('npk,pzykb->zybn', inv_real, averaged, precision=highest)
    result = result * (1.0 / 32768.0) * taper_window[:, None, None] * taper_window
    padding = jnp.zeros((depth, height, 1, 16), result.dtype)
    merged = jnp.concatenate([result[..., :16], padding], axis=2) + jnp.concatenate([padding, result[..., 16:]], axis=2)
    return merged.reshape(depth, height, width_x)

def filter_tile(extended, first_row, col_weight, shells):
    tables = make_tables()
    onehot = (jnp.arange(SHELLS, dtype=jnp.int32)[:, None] == shells.reshape(-1)[None, :]).astype(jnp.float32)
    box_rows = extended.shape[2] // 16 - 1

    def one_row(row_index):
        strip = lax.dynamic_slice_in_dim(extended, row_index * 16, 32, axis=2)
        row_factor = jnp.where(row_index == 0, first_row, 1.0)
        return filter_strip(strip * row_factor, onehot, tables, col_weight)
    strips = lax.map(one_row, jnp.arange(box_rows, dtype=jnp.int32))
    depth = strips.shape[1]
    width_x = strips.shape[3]
    padding = jnp.zeros((1, depth, 16, width_x), strips.dtype)
    summed = jnp.concatenate([strips[:, :, :16], padding], axis=0) + jnp.concatenate([padding, strips[:, :, 16:]], axis=0)
    summed = jnp.transpose(summed, (1, 0, 2, 3))
    return summed.reshape(depth, (box_rows + 1) * 16, width_x)

def reference(even_half, odd_half, slab_slices, shells):
    stacked = jnp.stack([even_half, odd_half])
    volume = jnp.zeros_like(stacked).at[:, slab_slices].set(stacked)
    padded = jnp.pad(volume, ((0, 0), (0, 0), (0, 16), (0, 16)))
    summed = filter_tile(padded, 1.0, jnp.ones((X // 16,), jnp.float32), shells)
    return summed[:, :Y, :X]
```

```python
import functools
import math

import jax
import jax.numpy as jnp
import ml_dtypes
import numpy as np
from jax import lax
from jax.experimental import pallas as pl
from jax.experimental.pallas import tpu as pltpu
from jax.sharding import PartitionSpec as P

SHELLS = 17
HALF = 17
F32 = jnp.float32
BF16 = jnp.bfloat16


def split_np(m):
    m = np.asarray(m, np.float64)
    hi = m.astype(np.float32).astype(ml_dtypes.bfloat16)
    lo = (m - hi.astype(np.float64)).astype(np.float32).astype(ml_dtypes.bfloat16)
    return hi, lo


def split(x):
    hi = x.astype(BF16)
    return hi, (x - hi.astype(F32)).astype(BF16)


def dot(a, b):
    return jnp.dot(a, b, preferred_element_type=F32)


def tables():
    n = np.arange(32)
    ang = 2.0 * np.pi / 32.0 * (n[:, None] * n[None, :] % 32)
    c, s = np.cos(ang), np.sin(ang)
    h = np.sin(np.pi * (n + 0.5) / 32.0)
    fx = np.zeros((2, 256, 2, 8, 32))
    ix = np.zeros((2, 8, 32, 2, 256))
    for b in range(8):
        v = slice(16 * b, 16 * b + 32)
        ch, sh = h[:, None] * c, h[:, None] * s
        fx[0, v, 0, b], fx[0, v, 1, b] = ch, -sh
        fx[1, v, 0, b], fx[1, v, 1, b] = sh, ch
        ix[0, b, :, 0, v], ix[0, b, :, 1, v] = ch.T, sh.T
        ix[1, b, :, 0, v], ix[1, b, :, 1, v] = -sh.T, ch.T
    fx = fx.reshape(512, 512)
    ix = ix.reshape(512, 512)
    fy = np.block([[c, s], [-s, c]]) * np.concatenate([h, h])[None, :]
    scale = 0.5 / 32768.0
    iy = np.block([[c, -s], [s, c]]) * (scale * np.concatenate([h, h]))[:, None]
    iz = np.concatenate([c[:, :17], -s[:, 1:16]], axis=1)
    iz = np.kron(iz, np.eye(8))
    out = []
    for m, axis in ((fx, 0), (fy, 1), (iy, 1), (ix, 0), (iz, 1)):
        hi, lo = split_np(m)
        out.append(np.concatenate([hi, lo, hi], axis=axis))
    return out


def z_forward(slab_slices):
    kz = jnp.arange(HALF, dtype=jnp.int32)
    step = kz[:, None] * slab_slices[None, :] % 32
    n = np.arange(32)
    table = np.stack([np.cos(2 * np.pi * n / 32), -np.sin(2 * np.pi * n / 32)])
    hi, lo = split_np(table)
    pick = (step[:, :, None] == jnp.arange(32, dtype=jnp.int32)).astype(F32)
    parts = []
    for t in (hi, lo):
        t = jnp.asarray(t.astype(np.float32))
        m = jnp.sum(pick[None] * t[:, None, None, :], axis=3).reshape(2 * HALF, 32)
        m = m[:, None, :, None] * jnp.eye(8, dtype=F32)[None, :, None, :]
        parts.append(m.reshape(2 * HALF * 8, 256).astype(BF16))
    return jnp.concatenate([parts[0], parts[1], parts[0]], axis=1)


def shell_masks(shells):
    front = shells[:HALF]
    back = jnp.roll(shells[::-1, ::-1, ::-1], (1, 1, 1), (0, 1, 2))[:HALF]
    kz = jnp.arange(HALF, dtype=jnp.int32)
    back = jnp.where(((kz > 0) & (kz < 16))[:, None, None], back, -1)
    front = front.reshape(HALF * 32, 32)
    back = back.reshape(HALF * 32, 32)
    s = jnp.arange(SHELLS, dtype=jnp.int32)

    def count(a, b, s):
        return ((a == s).astype(F32) + (b == s).astype(F32)).astype(BF16)

    wide = count(front[:, None, :], back[:, None, :], s[None, :, None])
    tall = count(front.T[None], back.T[None], s[:, None, None])
    return tall.reshape(SHELLS * 32, HALF * 32), wide.reshape(HALF * 32, SHELLS * 32)


def filter_kernel(ext, fz, fx, fy, iy, ix, iz, tall, wide, out, a_s, bhi, blo, avg, phi, plo, vox, c_s):
    for h in range(2):
        for o in range(4):
            hi, lo = split(ext[h, :, 8 * o : 8 * o + 8, :].reshape(256, 384))
            r = dot(fz[...], jnp.concatenate([hi, hi, lo], axis=0))
            a_s[h, :, 8 * o : 8 * o + 8, :] = r.reshape(2 * HALF, 8, 384)
    for h in range(2):
        for g in range(2):
            cols = slice(128 * g, 128 * g + 256)
            rhi, rlo = split(a_s[h, :HALF, :, cols].reshape(HALF * 32, 256))
            ihi, ilo = split(a_s[h, HALF:, :, cols].reshape(HALF * 32, 256))
            r = dot(jnp.concatenate([rhi, ihi, rhi, ihi, rlo, ilo], axis=1), fx[...])
            hi, lo = split(r)
            lanes = slice(256 * g, 256 * g + 256)
            bhi[h, :, :32, lanes] = hi[:, :256].reshape(HALF, 32, 256)
            bhi[h, :, 32:, lanes] = hi[:, 256:].reshape(HALF, 32, 256)
            blo[h, :, :32, lanes] = lo[:, :256].reshape(HALF, 32, 256)
            blo[h, :, 32:, lanes] = lo[:, 256:].reshape(HALF, 32, 256)

    def y_forward(kz, carry):
        spec = []
        for h in range(2):
            hi = bhi[h, kz]
            spec.append(dot(fy[...], jnp.concatenate([hi, hi, blo[h, kz]], axis=0)))
        e, o = spec
        avg[kz] = e + o
        for p, (x, y) in enumerate(((e, o), (e, e), (o, o))):
            hi, lo = split(x[:32] * y[:32] + x[32:] * y[32:])
            phi[kz, :, 512 * p : 512 * p + 512] = hi
            plo[kz, :, 512 * p : 512 * p + 512] = lo
        return carry

    lax.fori_loop(0, HALF, y_forward, 0)
    rows = SHELLS * 32
    same = lax.broadcasted_iota(jnp.int32, (32, 512), 0) == (
        lax.broadcasted_iota(jnp.int32, (32, 512), 1) % 32
    )
    group = (
        lax.broadcasted_iota(jnp.int32, (512, 512), 0) // 32
        == lax.broadcasted_iota(jnp.int32, (512, 512), 1) // 32
    ).astype(F32)
    sums = []
    for p in range(3):
        lanes = slice(512 * p, 512 * p + 512)
        t = dot(tall[...], phi[:, :, lanes].reshape(rows, 512))
        t = t + dot(tall[...], plo[:, :, lanes].reshape(rows, 512))
        t = jnp.sum(jnp.where(same[None], t.reshape(SHELLS, 32, 512), 0.0), axis=1)
        sums.append(jnp.dot(t, group, precision=lax.Precision.HIGHEST, preferred_element_type=F32))
    corr = sums[0] / jnp.sqrt(sums[1] * sums[2] + 1e-06)
    pos = jnp.maximum(corr, 0.0)
    w = 2.0 * pos / (1.0 + pos)
    w = jnp.where(same[None], w[:, None, :], 0.0).reshape(rows, 512)
    hi, lo = split(w)
    vox[...] = (dot(wide[...], hi) + dot(wide[...], lo)).reshape(HALF, 32, 512)

    def y_inverse(kz, carry):
        v = vox[kz]
        hi, lo = split(avg[kz] * jnp.concatenate([v, v], axis=0))
        r = dot(iy[...], jnp.concatenate([hi, hi, lo], axis=0))
        hi, lo = split(r)
        bhi[0, kz] = hi
        blo[0, kz] = lo
        return carry

    lax.fori_loop(0, HALF, y_inverse, 0)
    parts = []
    for g in range(2):
        lanes = slice(256 * g, 256 * g + 256)
        rhi = bhi[0, :, :32, lanes].reshape(rows, 256)
        ihi = bhi[0, :, 32:, lanes].reshape(rows, 256)
        rlo = blo[0, :, :32, lanes].reshape(rows, 256)
        ilo = blo[0, :, 32:, lanes].reshape(rows, 256)
        parts.append(dot(jnp.concatenate([rhi, ihi, rhi, ihi, rlo, ilo], axis=1), ix[...]))
    for q in range(2):
        first = parts[0][:, 256 * q : 256 * q + 256]
        second = parts[1][:, 256 * q : 256 * q + 256]
        planes = slice(HALF * q, HALF * q + HALF)
        c_s[planes, :, :128] = first[:, :128].reshape(HALF, 32, 128)
        c_s[planes, :, 128:256] = (first[:, 128:] + second[:, :128]).reshape(HALF, 32, 128)
        c_s[planes, :, 256:] = second[:, 128:].reshape(HALF, 32, 128)
    for o in range(4):
        block = slice(8 * o, 8 * o + 8)
        x = jnp.concatenate([c_s[:HALF, block, :], c_s[HALF + 1 : 2 * HALF - 1, block, :]], axis=0)
        hi, lo = split(x.reshape(256, 384))
        r = dot(iz[...], jnp.concatenate([hi, hi, lo], axis=0))
        out[:, block, :] = r.reshape(32, 8, 384)


def filter_tile(ext, slab_slices, shells):
    fx, fy, iy, ix, iz = [jnp.asarray(t) for t in tables()]
    tall, wide = shell_masks(shells)
    args = (ext, z_forward(slab_slices), fx, fy, iy, ix, iz, tall, wide)
    return pl.pallas_call(
        filter_kernel,
        out_shape=jax.ShapeDtypeStruct((32, 32, 384), F32),
        in_specs=[pl.BlockSpec(memory_space=pltpu.VMEM)] * len(args),
        out_specs=pl.BlockSpec(memory_space=pltpu.VMEM),
        scratch_shapes=[
            pltpu.VMEM((2, 2 * HALF, 32, 384), F32),
            pltpu.VMEM((2, HALF, 64, 512), BF16),
            pltpu.VMEM((2, HALF, 64, 512), BF16),
            pltpu.VMEM((HALF, 64, 512), F32),
            pltpu.VMEM((HALF, 32, 1536), BF16),
            pltpu.VMEM((HALF, 32, 1536), BF16),
            pltpu.VMEM((HALF, 32, 512), F32),
            pltpu.VMEM((2 * HALF, 32, 384), F32),
        ],
        compiler_params=pltpu.CompilerParams(vmem_limit_bytes=56 * 1024 * 1024),
    )(*args)


def from_behind(block, axis, distance):
    devices = range(lax.axis_size(axis))
    route = [(i - distance, i) for i in devices if i - distance in devices]
    return lax.ppermute(block, axis, route)


def on_device(even_half, odd_half, slab_slices, shells):
    halves_pair = jnp.stack([even_half, odd_half])
    tile_pair = lax.all_to_all(
        lax.all_to_all(halves_pair, "gy", split_axis=2, concat_axis=3, tiled=True),
        "gx",
        split_axis=3,
        concat_axis=1,
        tiled=True,
    )
    rows_tile = tile_pair.shape[2]
    cols_tile = tile_pair.shape[3]
    upper_cols = from_behind(tile_pair[:, :, :, :16], "gx", -1)
    extended = jnp.concatenate([tile_pair, upper_cols], axis=3)
    upper_rows = from_behind(extended, "gy", -1)
    extended = jnp.concatenate([extended, upper_rows], axis=2)
    extended = jnp.pad(extended, ((0, 0), (0, 0), (0, 0), (0, 112)))
    summed = filter_tile(extended, slab_slices, shells)[:, :, : cols_tile + 16]
    spill_rows = from_behind(summed[:, rows_tile:, :], "gy", 1)
    summed = jnp.concatenate([summed[:, :16, :] + spill_rows, summed[:, 16:rows_tile, :]], axis=1)
    spill_cols = from_behind(summed[:, :, cols_tile:], "gx", 1)
    filtered = jnp.concatenate([summed[:, :, :16] + spill_cols, summed[:, :, 16:cols_tile]], axis=2)
    return filtered


def solution(mesh):
    in_specs = (P("gx", None, "gy"), P("gx", None, "gy"), P(), P())
    out_specs = P(None, "gy", "gx")
    return jax.shard_map(
        on_device, mesh=mesh, in_specs=in_specs, out_specs=out_specs, check_vma=False
    )
```

```python
import functools

import jax
import jax.numpy as jnp
import ml_dtypes
import numpy as np
from jax import lax
from jax.experimental import pallas as pl
from jax.experimental.pallas import tpu as pltpu
from jax.sharding import PartitionSpec as P

SHELLS = 17
HALF = 17
F32 = jnp.float32
BF16 = jnp.bfloat16


def split_np(m):
    m = np.asarray(m, np.float64)
    hi = m.astype(np.float32).astype(ml_dtypes.bfloat16)
    lo = (m - hi.astype(np.float64)).astype(np.float32).astype(ml_dtypes.bfloat16)
    return hi, lo


def split(x):
    hi = x.astype(BF16)
    return hi, (x - hi.astype(F32)).astype(BF16)


def dot(a, b):
    return jnp.dot(a, b, preferred_element_type=F32)


def tables():
    n = np.arange(32)
    ang = 2.0 * np.pi / 32.0 * (n[:, None] * n[None, :] % 32)
    c, s = np.cos(ang), np.sin(ang)
    h = np.sin(np.pi * (n + 0.5) / 32.0)
    fx = np.zeros((2, 256, 2, 8, 32))
    ix = np.zeros((2, 8, 32, 2, 256))
    for b in range(8):
        v = slice(16 * b, 16 * b + 32)
        ch, sh = h[:, None] * c, h[:, None] * s
        fx[0, v, 0, b], fx[0, v, 1, b] = ch, -sh
        fx[1, v, 0, b], fx[1, v, 1, b] = sh, ch
        ix[0, b, :, 0, v], ix[0, b, :, 1, v] = ch.T, sh.T
        ix[1, b, :, 0, v], ix[1, b, :, 1, v] = -sh.T, ch.T
    fx = fx.reshape(512, 512)
    ix = ix.reshape(512, 512)
    fy = np.block([[c, s], [-s, c]]) * np.concatenate([h, h])[None, :]
    scale = 0.5 / 32768.0
    iy = np.block([[c, -s], [s, c]]) * (scale * np.concatenate([h, h]))[:, None]
    iz = np.concatenate([c[:, :17], -s[:, 1:16]], axis=1)
    iz = np.kron(iz, np.eye(8))
    out = []
    for m, axis in ((fx, 0), (fy, 1), (iy, 1), (ix, 0), (iz, 1)):
        hi, lo = split_np(m)
        out.append(np.concatenate([hi, lo, hi], axis=axis))
    return out


def shell_pair(shells):
    front = shells[:HALF]
    back = jnp.roll(shells[::-1, ::-1, ::-1], (1, 1, 1), (0, 1, 2))[:HALF]
    kz = jnp.arange(HALF, dtype=jnp.int32)
    back = jnp.where(((kz > 0) & (kz < 16))[:, None, None], back, -1)
    pair = jnp.stack([front.reshape(HALF * 32, 32), back.reshape(HALF * 32, 32)])
    return jnp.tile(pair, (1, 1, 4)), jnp.transpose(pair, (0, 2, 1))


def head_lanes(x, k):
    lane = lax.broadcasted_iota(jnp.int32, x.shape, 1)
    return jnp.where(lane < 16, pltpu.roll(x, (128 - 16 * k) % 128, 1) if k else x, 0.0)


def place_lanes(x, k):
    lane = lax.broadcasted_iota(jnp.int32, x.shape, 1)
    x = jnp.where(lane < 16, x, 0.0)
    return pltpu.roll(x, 16 * k, 1) if k else x


def filter_kernel(
    main, packed, slab, pairs, turned, zt, fx, fy, iy, ix, iz, out, tail_out,
    rim, tall, wide, a_s, bhi, blo, avg, phi, plo, vox, c_s,
):
    for i in range(5):
        shell = 4 * i + lax.broadcasted_iota(jnp.int32, (HALF * 32, 128), 1) // 32
        m = (pairs[0] == shell).astype(F32) + (pairs[1] == shell).astype(F32)
        wide[:, 128 * i : 128 * i + 128] = m.astype(BF16)
    for s in range(SHELLS):
        m = (turned[0] == s).astype(F32) + (turned[1] == s).astype(F32)
        tall[32 * s : 32 * s + 32, :] = m.astype(BF16)
    place = lax.broadcasted_iota(jnp.int32, (256, 256), 0)
    place = (place // 8 == slab[...]) & (
        place % 8 == lax.broadcasted_iota(jnp.int32, (256, 256), 1) % 8
    )
    place = place.astype(F32).astype(BF16)
    zhi = dot(zt[0], place).astype(BF16)
    zlo = dot(zt[1], place).astype(BF16)
    fz = jnp.concatenate([zhi, zlo, zhi], axis=1)
    slots = 32 // packed.shape[0]
    for s in range(packed.shape[0]):
        for h in range(2):
            for k in range(slots):
                rim[h, slots * s + k] = head_lanes(packed[s, h], k)
    for h in range(2):
        for o in range(4):
            block = slice(8 * o, 8 * o + 8)
            x = jnp.concatenate(
                [main[0, h, :, block, :], main[1, h, :, block, :], rim[h, :, block, :]], axis=2
            )
            hi, lo = split(x.reshape(256, 384))
            r = dot(fz, jnp.concatenate([hi, hi, lo], axis=0))
            a_s[h, :, 8 * o : 8 * o + 8, :] = r.reshape(2 * HALF, 8, 384)
    for h in range(2):
        for g in range(2):
            cols = slice(128 * g, 128 * g + 256)
            rhi, rlo = split(a_s[h, :HALF, :, cols].reshape(HALF * 32, 256))
            ihi, ilo = split(a_s[h, HALF:, :, cols].reshape(HALF * 32, 256))
            r = dot(jnp.concatenate([rhi, ihi, rhi, ihi, rlo, ilo], axis=1), fx[...])
            hi, lo = split(r)
            lanes = slice(256 * g, 256 * g + 256)
            bhi[h, :, :32, lanes] = hi[:, :256].reshape(HALF, 32, 256)
            bhi[h, :, 32:, lanes] = hi[:, 256:].reshape(HALF, 32, 256)
            blo[h, :, :32, lanes] = lo[:, :256].reshape(HALF, 32, 256)
            blo[h, :, 32:, lanes] = lo[:, 256:].reshape(HALF, 32, 256)

    def y_forward(kz, carry):
        spec = []
        for h in range(2):
            hi = bhi[h, kz]
            spec.append(dot(fy[...], jnp.concatenate([hi, hi, blo[h, kz]], axis=0)))
        e, o = spec
        avg[kz] = e + o
        for p, (x, y) in enumerate(((e, o), (e, e), (o, o))):
            hi, lo = split(x[:32] * y[:32] + x[32:] * y[32:])
            phi[kz, :, 512 * p : 512 * p + 512] = hi
            plo[kz, :, 512 * p : 512 * p + 512] = lo
        return carry

    lax.fori_loop(0, HALF, y_forward, 0)
    rows = SHELLS * 32
    same = lax.broadcasted_iota(jnp.int32, (32, 512), 0) == (
        lax.broadcasted_iota(jnp.int32, (32, 512), 1) % 32
    )
    group = (
        lax.broadcasted_iota(jnp.int32, (512, 512), 0) // 32
        == lax.broadcasted_iota(jnp.int32, (512, 512), 1) // 32
    ).astype(F32)
    sums = []
    for p in range(3):
        lanes = slice(512 * p, 512 * p + 512)
        t = dot(tall[...], phi[:, :, lanes].reshape(rows, 512))
        t = t + dot(tall[...], plo[:, :, lanes].reshape(rows, 512))
        t = jnp.sum(jnp.where(same[None], t.reshape(SHELLS, 32, 512), 0.0), axis=1)
        sums.append(jnp.dot(t, group, precision=lax.Precision.HIGHEST, preferred_element_type=F32))
    corr = sums[0] / jnp.sqrt(sums[1] * sums[2] + 1e-06)
    pos = jnp.maximum(corr, 0.0)
    w = 2.0 * pos / (1.0 + pos)
    w = jnp.where(same[None], w[:, None, :], 0.0).reshape(rows, 512)
    w = jnp.concatenate([w, jnp.zeros((640 - rows, 512), F32)], axis=0)
    hi, lo = split(w)
    vox[...] = (dot(wide[...], hi) + dot(wide[...], lo)).reshape(HALF, 32, 512)

    def y_inverse(kz, carry):
        v = vox[kz]
        hi, lo = split(avg[kz] * jnp.concatenate([v, v], axis=0))
        r = dot(iy[...], jnp.concatenate([hi, hi, lo], axis=0))
        hi, lo = split(r)
        bhi[0, kz] = hi
        blo[0, kz] = lo
        return carry

    lax.fori_loop(0, HALF, y_inverse, 0)
    parts = []
    for g in range(2):
        lanes = slice(256 * g, 256 * g + 256)
        rhi = bhi[0, :, :32, lanes].reshape(rows, 256)
        ihi = bhi[0, :, 32:, lanes].reshape(rows, 256)
        rlo = blo[0, :, :32, lanes].reshape(rows, 256)
        ilo = blo[0, :, 32:, lanes].reshape(rows, 256)
        parts.append(dot(jnp.concatenate([rhi, ihi, rhi, ihi, rlo, ilo], axis=1), ix[...]))
    for q in range(2):
        first = parts[0][:, 256 * q : 256 * q + 256]
        second = parts[1][:, 256 * q : 256 * q + 256]
        planes = slice(HALF * q, HALF * q + HALF)
        c_s[planes, :, :128] = first[:, :128].reshape(HALF, 32, 128)
        c_s[planes, :, 128:256] = (first[:, 128:] + second[:, :128]).reshape(HALF, 32, 128)
        c_s[planes, :, 256:] = second[:, 128:].reshape(HALF, 32, 128)
    for o in range(4):
        block = slice(8 * o, 8 * o + 8)
        x = jnp.concatenate([c_s[:HALF, block, :], c_s[HALF + 1 : 2 * HALF - 1, block, :]], axis=0)
        hi, lo = split(x.reshape(256, 384))
        r = dot(iz[...], jnp.concatenate([hi, hi, lo], axis=0))
        r = r.reshape(32, 8, 384)
        out[0, :, block, :] = r[:, :, :128]
        out[1, :, block, :] = r[:, :, 128:256]
        rim[0, :, block, :] = r[:, :, 256:]
    for q in range(4):
        tail_out[q] = sum(place_lanes(rim[0, 8 * q + k], k) for k in range(8))


def z_table():
    n = np.arange(32)
    ang = 2.0 * np.pi / 32.0 * (n[:, None] * n[None, :] % 32)
    m = np.concatenate([np.cos(ang)[:HALF], -np.sin(ang)[:HALF]], axis=0)
    return np.stack(split_np(np.kron(m, np.eye(8))))


def filter_tile(main, packed, slab_slices, shells):
    consts = [jnp.asarray(t) for t in tables()]
    pairs, turned = shell_pair(shells)
    slab = jnp.repeat(slab_slices, 8).reshape(1, 256)
    args = (main, packed, slab, pairs, turned, jnp.asarray(z_table()), *consts)
    vmem = pl.BlockSpec(memory_space=pltpu.VMEM)
    return pl.pallas_call(
        filter_kernel,
        out_shape=(
            jax.ShapeDtypeStruct((2, 32, 32, 128), F32),
            jax.ShapeDtypeStruct((4, 32, 128), F32),
        ),
        in_specs=[vmem] * len(args),
        out_specs=(vmem, vmem),
        scratch_shapes=[
            pltpu.VMEM((2, 32, 32, 128), F32),
            pltpu.VMEM((SHELLS * 32, HALF * 32), BF16),
            pltpu.VMEM((HALF * 32, 640), BF16),
            pltpu.VMEM((2, 2 * HALF, 32, 384), F32),
            pltpu.VMEM((2, HALF, 64, 512), BF16),
            pltpu.VMEM((2, HALF, 64, 512), BF16),
            pltpu.VMEM((HALF, 64, 512), F32),
            pltpu.VMEM((HALF, 32, 1536), BF16),
            pltpu.VMEM((HALF, 32, 1536), BF16),
            pltpu.VMEM((HALF, 32, 512), F32),
            pltpu.VMEM((2 * HALF, 32, 384), F32),
        ],
        compiler_params=pltpu.CompilerParams(vmem_limit_bytes=56 * 1024 * 1024),
    )(*args)


def remote(src, dst, send, recv, device):
    return pltpu.make_async_remote_copy(
        src_ref=src, dst_ref=dst, send_sem=send, recv_sem=recv,
        device_id=device, device_id_type=pl.DeviceIdType.MESH,
    )


def gather_kernel(
    G, N, even, odd, main, packed, stage, pack,
    send_a, recv_a, send_b, recv_b, send_h, recv_h, send_c, recv_c, send_d, recv_d,
):
    slots = 32 // N
    per = G // N
    g, s = lax.axis_index("gy"), lax.axis_index("gx")
    barrier = pltpu.get_barrier_semaphore()
    for i in range(1, G):
        pl.semaphore_signal(
            barrier, inc=1, device_id=(lax.rem(g + i, G), s), device_id_type=pl.DeviceIdType.MESH
        )
    for i in range(1, N):
        pl.semaphore_signal(
            barrier, inc=1, device_id=(g, lax.rem(s + i, N)), device_id_type=pl.DeviceIdType.MESH
        )
    pl.semaphore_wait(barrier, G + N - 2)

    def rows_of(k):
        return pl.ds(pl.multiple_of(16 * k, 16), 16)

    def copy_a(i, h):
        to = lax.rem(g + i, G)
        src = (even, odd)[h]
        return remote(
            src.at[:, rows_of(to), :], stage.at[i, h], send_a.at[i, h], recv_a.at[i, h], (to, s)
        )

    for i in range(1, G):
        for h in range(2):
            copy_a(i, h).start()
    stage[0, 0] = even[:, rows_of(g), :]
    stage[0, 1] = odd[:, rows_of(g), :]

    def source(i):
        g0 = lax.rem(g + G - i, G)
        return g0 // per, lax.rem(g0, per)

    def part(t, z, r):
        return main.at[t, :, pl.ds(slots * z, slots), pl.ds(r, 16), :]

    def copy_b(i):
        c, t = source(i)
        return remote(stage.at[i], part(t, s, 0), send_b.at[i], recv_b.at[s, t], (g, c))

    def local_b(i):
        t = source(i)[1]
        return pltpu.make_async_copy(stage.at[i], part(t, s, 0), send_b.at[i])

    def copy_h(i):
        c = source(i)[0] - 1
        return remote(
            pack.at[i], packed.at[s, :, pl.ds(0, 16), :], send_h.at[i], recv_h.at[s], (g, c)
        )

    for i in range(G):
        if i:
            for h in range(2):
                copy_a(i, h).wait_recv()
        c, t = source(i)

        @pl.when(c == s)
        def _():
            local_b(i).start()

        @pl.when(c != s)
        def _():
            copy_b(i).start()

        @pl.when((t == 0) & (c > 0))
        def _():
            for h in range(2):
                pack[i, h] = sum(place_lanes(stage[i, h, k], k) for k in range(slots))

        @pl.when((t == 0) & (c > 0) & (c != s + 1))
        def _():
            copy_h(i).start()

        @pl.when((t == 0) & (c > 0) & (c == s + 1))
        def _():
            packed[s, :, 0:16, :] = pack[i]

    for i in range(G):

        @pl.when(source(i)[0] == s)
        def _():
            local_b(i).wait()

    def copy_c(j, t):
        z = lax.rem(s + j, N)
        return remote(part(t, z, 0), part(t, z, 16), send_c.at[j, t], recv_c.at[j, t], (g - 1, s))

    def wait_b(j, t):
        z = lax.rem(s + j, N)
        remote(part(t, z, 0), part(t, z, 0), send_c.at[j, t], recv_b.at[z, t], (g, z)).wait_recv()

    order = [0] + [k for d in range(1, N) for k in (d, N - d)]
    order = list(dict.fromkeys(order))
    for j in order:
        for t in range(per):
            if j:
                wait_b(j, t)

            @pl.when(g > 0)
            def _():
                copy_c(j, t).start()

    @pl.when(s < N - 1)
    def _():
        for j in range(1, N):
            z = lax.rem(s + j, N)
            block = packed.at[z, :, pl.ds(0, 16), :]
            remote(block, block, send_d.at[0], recv_h.at[z], (g, z)).wait_recv()

    @pl.when(s == N - 1)
    def _():
        packed[:, :, 0:16, :] = jnp.zeros((N, 2, 16, 128), F32)

    def copy_d():
        return remote(
            packed.at[:, :, pl.ds(0, 16), :], packed.at[:, :, pl.ds(16, 16), :],
            send_d.at[0], recv_d.at[0], (g - 1, s),
        )

    @pl.when(g > 0)
    def _():
        copy_d().start()

    @pl.when(g == G - 1)
    def _():
        packed[:, :, 16:32, :] = jnp.zeros((N, 2, 16, 128), F32)
        main[:, :, :, 16:32, :] = jnp.zeros((per, 2, 32, 16, 128), F32)

    @pl.when(g < G - 1)
    def _():
        for j in order:
            for t in range(per):
                copy_c(j, t).wait_recv()
        copy_d().wait_recv()

    for i in range(1, G):
        for h in range(2):
            copy_a(i, h).wait_send()
    for i in range(G):
        c, t = source(i)

        @pl.when(c != s)
        def _():
            copy_b(i).wait_send()

        @pl.when((t == 0) & (c > 0) & (c != s + 1))
        def _():
            copy_h(i).wait_send()

    @pl.when(g > 0)
    def _():
        for j in order:
            for t in range(per):
                copy_c(j, t).wait_send()
        copy_d().wait_send()


def gather(even, odd):
    G, N = lax.axis_size("gy"), lax.axis_size("gx")
    slots, per = 32 // N, G // N
    vmem = pl.BlockSpec(memory_space=pltpu.VMEM)
    dma = pltpu.SemaphoreType.DMA
    return pl.pallas_call(
        functools.partial(gather_kernel, G, N),
        out_shape=(
            jax.ShapeDtypeStruct((per, 2, 32, 32, 128), F32),
            jax.ShapeDtypeStruct((N, 2, 32, 128), F32),
        ),
        in_specs=[vmem, vmem],
        out_specs=(vmem, vmem),
        scratch_shapes=[
            pltpu.VMEM((G, 2, slots, 16, 128), F32),
            pltpu.VMEM((G, 2, 16, 128), F32),
            dma((G, 2)), dma((G, 2)), dma((G,)), dma((N, per)), dma((G,)), dma((N,)),
            dma((N, per)), dma((N, per)), dma((1,)), dma((1,)),
        ],
        compiler_params=pltpu.CompilerParams(
            collective_id=0, has_side_effects=True, vmem_limit_bytes=32 * 1024 * 1024
        ),
    )(even, odd)


def spill_kernel(G, N, body, tail, out, rows, top, low, send, recv):
    g, s = lax.axis_index("gy"), lax.axis_index("gx")
    barrier = pltpu.get_barrier_semaphore()
    steps = ((1, 0), (0, 1), (1, 1))

    def ahead(dg, ds):
        return (g < G - dg) & (s < N - ds)

    def behind(dg, ds):
        return (g >= dg) & (s >= ds)

    for dg, ds in steps:

        @pl.when(ahead(dg, ds))
        def _():
            pl.semaphore_signal(
                barrier, inc=1, device_id=(g + dg, s + ds), device_id_type=pl.DeviceIdType.MESH
            )

        @pl.when(behind(dg, ds))
        def _():
            pl.semaphore_signal(
                barrier, inc=1, device_id=(g - dg, s - ds), device_id_type=pl.DeviceIdType.MESH
            )

    peers = sum(f(*d).astype(jnp.int32) for f in (ahead, behind) for d in steps)
    pl.semaphore_wait(barrier, peers)

    sources = (
        body.at[:, :, pl.ds(16, 16), :], tail.at[:, pl.ds(0, 16), :], tail.at[:, pl.ds(16, 16), :]
    )
    targets = (rows, top, low)

    def copy(k):
        dg, ds = steps[k]
        return remote(sources[k], targets[k], send.at[k], recv.at[k], (g + dg, s + ds))

    for k in range(3):

        @pl.when(ahead(*steps[k]))
        def _():
            copy(k).start()

        @pl.when(jnp.logical_not(behind(*steps[k])))
        def _():
            targets[k][...] = jnp.zeros(targets[k].shape, F32)

    for k in range(3):

        @pl.when(behind(*steps[k]))
        def _():
            copy(k).wait_recv()

    for z in range(32):
        q = z // 8
        rim = head_lanes(top[q] + low[q], z % 8)
        out[z, :, :128] = body[0, z, :16, :] + rows[0, z] + rim
        out[z, :, 128:] = body[1, z, :16, :] + rows[1, z]
    for k in range(3):

        @pl.when(ahead(*steps[k]))
        def _():
            copy(k).wait_send()


def spill(body, tail):
    G, N = lax.axis_size("gy"), lax.axis_size("gx")
    vmem = pl.BlockSpec(memory_space=pltpu.VMEM)
    dma = pltpu.SemaphoreType.DMA
    return pl.pallas_call(
        functools.partial(spill_kernel, G, N),
        out_shape=jax.ShapeDtypeStruct((32, 16, 256), F32),
        in_specs=[vmem, vmem],
        out_specs=vmem,
        scratch_shapes=[
            pltpu.VMEM((2, 32, 16, 128), F32),
            pltpu.VMEM((4, 16, 128), F32),
            pltpu.VMEM((4, 16, 128), F32),
            dma((3,)), dma((3,)),
        ],
        compiler_params=pltpu.CompilerParams(
            collective_id=1, has_side_effects=True, vmem_limit_bytes=32 * 1024 * 1024
        ),
    )(body, tail)


def on_device(even_half, odd_half, slab_slices, shells):
    main, packed = gather(even_half, odd_half)
    body, tail = filter_tile(main, packed, slab_slices, shells)
    return spill(body, tail)


def solution(mesh):
    in_specs = (P("gx", None, "gy"), P("gx", None, "gy"), P(), P())
    out_specs = P(None, "gy", "gx")
    return jax.shard_map(
        on_device, mesh=mesh, in_specs=in_specs, out_specs=out_specs, check_vma=False
    )
```

```python
import functools

import jax
import jax.numpy as jnp
import ml_dtypes
import numpy as np
from jax import lax
from jax.experimental import pallas as pl
from jax.experimental.pallas import tpu as pltpu
from jax.sharding import PartitionSpec as P

SHELLS = 17
HALF = 17
F32 = jnp.float32
BF16 = jnp.bfloat16


def split_np(m):
    m = np.asarray(m, np.float64)
    hi = m.astype(np.float32).astype(ml_dtypes.bfloat16)
    lo = (m - hi.astype(np.float64)).astype(np.float32).astype(ml_dtypes.bfloat16)
    return hi, lo


def split(x):
    hi = x.astype(BF16)
    return hi, (x - hi.astype(F32)).astype(BF16)


def dot(a, b):
    return jnp.dot(a, b, preferred_element_type=F32)


def tables():
    n = np.arange(32)
    ang = 2.0 * np.pi / 32.0 * (n[:, None] * n[None, :] % 32)
    c, s = np.cos(ang), np.sin(ang)
    h = np.sin(np.pi * (n + 0.5) / 32.0)
    fx = np.zeros((2, 256, 2, 8, 32))
    ix = np.zeros((2, 8, 32, 2, 256))
    for b in range(8):
        v = slice(16 * b, 16 * b + 32)
        ch, sh = h[:, None] * c, h[:, None] * s
        fx[0, v, 0, b], fx[0, v, 1, b] = ch, -sh
        fx[1, v, 0, b], fx[1, v, 1, b] = sh, ch
        ix[0, b, :, 0, v], ix[0, b, :, 1, v] = ch.T, sh.T
        ix[1, b, :, 0, v], ix[1, b, :, 1, v] = -sh.T, ch.T
    fx = fx.reshape(512, 512)
    ix = ix.reshape(512, 512)
    fy = np.block([[c, s], [-s, c]]) * np.concatenate([h, h])[None, :]
    scale = 0.5 / 32768.0
    iy = np.block([[c, -s], [s, c]]) * (scale * np.concatenate([h, h]))[:, None]
    iz = np.concatenate([c[:, :17], -s[:, 1:16]], axis=1)
    iz = np.kron(iz, np.eye(8))
    out = []
    for m, axis in ((fx, 0), (fy, 1), (iy, 1), (ix, 0), (iz, 1)):
        hi, lo = split_np(m)
        out.append(np.concatenate([hi, lo, hi], axis=axis))
    return out


def head_lanes(x, k):
    lane = lax.broadcasted_iota(jnp.int32, x.shape, 1)
    return jnp.where(lane < 16, pltpu.roll(x, (128 - 16 * k) % 128, 1) if k else x, 0.0)


def place_lanes(x, k):
    lane = lax.broadcasted_iota(jnp.int32, x.shape, 1)
    x = jnp.where(lane < 16, x, 0.0)
    return pltpu.roll(x, 16 * k, 1) if k else x


def filter_kernel(
    main, packed, slab, shells, zt, fx, fy, iy, ix, iz, out, tail_out,
    rim, tall, wide, a_s, bhi, blo, avg, phi, plo, vox, c_s,
):
    def iota(shape, axis):
        return lax.broadcasted_iota(jnp.int32, shape, axis)

    def exact(mask):
        return mask.astype(F32).astype(BF16)

    numbers = shells[...].astype(F32).astype(BF16)
    tile = exact(iota((32, 128), 1) % 32 == iota((32, 128), 0))
    tile_back = exact((32 - iota((32, 128), 1) % 32) % 32 == iota((32, 128), 0))
    turn = exact(iota((32, 32), 0) == iota((32, 32), 1))
    turn_back = exact((32 - iota((32, 32), 0)) % 32 == iota((32, 32), 1))
    front = dot(numbers[: HALF * 32], tile)
    flipped = dot(numbers, tile_back).astype(BF16)
    none = jnp.full((32, 128), -1.0, F32)
    back = [none] + [dot(turn_back, flipped[32 * (32 - k) : 32 * (33 - k)]) for k in range(1, 16)]
    back = jnp.concatenate(back + [none], axis=0)
    sides = (((1,), (1,)), ((), ()))
    front_t = lax.dot_general(
        turn, front[:, :32].astype(BF16), sides, preferred_element_type=F32
    )
    back_t = lax.dot_general(turn, back[:, :32].astype(BF16), sides, preferred_element_type=F32)
    for i in range(5):
        shell = (4 * i + iota((HALF * 32, 128), 1) // 32).astype(F32)
        m = (front == shell).astype(F32) + (back == shell).astype(F32)
        wide[:, 128 * i : 128 * i + 128] = m.astype(BF16)
    for s in range(SHELLS):
        m = (front_t == s).astype(F32) + (back_t == s).astype(F32)
        tall[32 * s : 32 * s + 32, :] = m.astype(BF16)
    spread = exact(iota((32, 256), 1) // 8 == iota((32, 256), 0))
    slices = jnp.broadcast_to(slab[...].astype(F32), (8, 32)).astype(BF16)
    slices = dot(slices, spread)[0:1]
    place = iota((256, 256), 0)
    place = exact(
        ((place // 8).astype(F32) == slices) & (place % 8 == iota((256, 256), 1) % 8)
    )
    zhi = dot(zt[0], place).astype(BF16)
    zlo = dot(zt[1], place).astype(BF16)
    fz = jnp.concatenate([zhi, zlo, zhi], axis=1)
    slots = 32 // packed.shape[0]
    for s in range(packed.shape[0]):
        for h in range(2):
            for k in range(slots):
                rim[h, slots * s + k] = head_lanes(packed[s, h], k)
    for h in range(2):
        for o in range(4):
            block = slice(8 * o, 8 * o + 8)
            x = jnp.concatenate(
                [main[0, h, :, block, :], main[1, h, :, block, :], rim[h, :, block, :]], axis=2
            )
            hi, lo = split(x.reshape(256, 384))
            r = dot(fz, jnp.concatenate([hi, hi, lo], axis=0))
            a_s[h, :, 8 * o : 8 * o + 8, :] = r.reshape(2 * HALF, 8, 384)
    for h in range(2):
        for g in range(2):
            cols = slice(128 * g, 128 * g + 256)
            rhi, rlo = split(a_s[h, :HALF, :, cols].reshape(HALF * 32, 256))
            ihi, ilo = split(a_s[h, HALF:, :, cols].reshape(HALF * 32, 256))
            r = dot(jnp.concatenate([rhi, ihi, rhi, ihi, rlo, ilo], axis=1), fx[...])
            hi, lo = split(r)
            lanes = slice(256 * g, 256 * g + 256)
            bhi[h, :, :32, lanes] = hi[:, :256].reshape(HALF, 32, 256)
            bhi[h, :, 32:, lanes] = hi[:, 256:].reshape(HALF, 32, 256)
            blo[h, :, :32, lanes] = lo[:, :256].reshape(HALF, 32, 256)
            blo[h, :, 32:, lanes] = lo[:, 256:].reshape(HALF, 32, 256)

    def y_forward(kz, carry):
        spec = []
        for h in range(2):
            hi = bhi[h, kz]
            spec.append(dot(fy[...], jnp.concatenate([hi, hi, blo[h, kz]], axis=0)))
        e, o = spec
        avg[kz] = e + o
        for p, (x, y) in enumerate(((e, o), (e, e), (o, o))):
            hi, lo = split(x[:32] * y[:32] + x[32:] * y[32:])
            phi[kz, :, 512 * p : 512 * p + 512] = hi
            plo[kz, :, 512 * p : 512 * p + 512] = lo
        return carry

    lax.fori_loop(0, HALF, y_forward, 0)
    rows = SHELLS * 32
    same = lax.broadcasted_iota(jnp.int32, (32, 512), 0) == (
        lax.broadcasted_iota(jnp.int32, (32, 512), 1) % 32
    )
    group = (
        lax.broadcasted_iota(jnp.int32, (512, 512), 0) // 32
        == lax.broadcasted_iota(jnp.int32, (512, 512), 1) // 32
    ).astype(F32)
    sums = []
    for p in range(3):
        lanes = slice(512 * p, 512 * p + 512)
        t = dot(tall[...], phi[:, :, lanes].reshape(rows, 512))
        t = t + dot(tall[...], plo[:, :, lanes].reshape(rows, 512))
        t = jnp.sum(jnp.where(same[None], t.reshape(SHELLS, 32, 512), 0.0), axis=1)
        sums.append(jnp.dot(t, group, precision=lax.Precision.HIGHEST, preferred_element_type=F32))
    corr = sums[0] / jnp.sqrt(sums[1] * sums[2] + 1e-06)
    pos = jnp.maximum(corr, 0.0)
    w = 2.0 * pos / (1.0 + pos)
    w = jnp.where(same[None], w[:, None, :], 0.0).reshape(rows, 512)
    w = jnp.concatenate([w, jnp.zeros((640 - rows, 512), F32)], axis=0)
    hi, lo = split(w)
    vox[...] = (dot(wide[...], hi) + dot(wide[...], lo)).reshape(HALF, 32, 512)

    def y_inverse(kz, carry):
        v = vox[kz]
        hi, lo = split(avg[kz] * jnp.concatenate([v, v], axis=0))
        r = dot(iy[...], jnp.concatenate([hi, hi, lo], axis=0))
        hi, lo = split(r)
        bhi[0, kz] = hi
        blo[0, kz] = lo
        return carry

    lax.fori_loop(0, HALF, y_inverse, 0)
    parts = []
    for g in range(2):
        lanes = slice(256 * g, 256 * g + 256)
        rhi = bhi[0, :, :32, lanes].reshape(rows, 256)
        ihi = bhi[0, :, 32:, lanes].reshape(rows, 256)
        rlo = blo[0, :, :32, lanes].reshape(rows, 256)
        ilo = blo[0, :, 32:, lanes].reshape(rows, 256)
        parts.append(dot(jnp.concatenate([rhi, ihi, rhi, ihi, rlo, ilo], axis=1), ix[...]))
    for q in range(2):
        first = parts[0][:, 256 * q : 256 * q + 256]
        second = parts[1][:, 256 * q : 256 * q + 256]
        planes = slice(HALF * q, HALF * q + HALF)
        c_s[planes, :, :128] = first[:, :128].reshape(HALF, 32, 128)
        c_s[planes, :, 128:256] = (first[:, 128:] + second[:, :128]).reshape(HALF, 32, 128)
        c_s[planes, :, 256:] = second[:, 128:].reshape(HALF, 32, 128)
    for o in range(4):
        block = slice(8 * o, 8 * o + 8)
        x = jnp.concatenate([c_s[:HALF, block, :], c_s[HALF + 1 : 2 * HALF - 1, block, :]], axis=0)
        hi, lo = split(x.reshape(256, 384))
        r = dot(iz[...], jnp.concatenate([hi, hi, lo], axis=0))
        r = r.reshape(32, 8, 384)
        out[0, :, block, :] = r[:, :, :128]
        out[1, :, block, :] = r[:, :, 128:256]
        rim[0, :, block, :] = r[:, :, 256:]
    for q in range(4):
        tail_out[q] = sum(place_lanes(rim[0, 8 * q + k], k) for k in range(8))


def z_table():
    n = np.arange(32)
    ang = 2.0 * np.pi / 32.0 * (n[:, None] * n[None, :] % 32)
    m = np.concatenate([np.cos(ang)[:HALF], -np.sin(ang)[:HALF]], axis=0)
    return np.stack(split_np(np.kron(m, np.eye(8))))


def filter_tile(main, packed, slab_slices, shells):
    consts = [jnp.asarray(t) for t in tables()]
    args = (main, packed, slab_slices.reshape(1, 32), shells.reshape(1024, 32), jnp.asarray(z_table()), *consts)
    vmem = pl.BlockSpec(memory_space=pltpu.VMEM)
    return pl.pallas_call(
        filter_kernel,
        out_shape=(
            jax.ShapeDtypeStruct((2, 32, 32, 128), F32),
            jax.ShapeDtypeStruct((4, 32, 128), F32),
        ),
        in_specs=[vmem] * len(args),
        out_specs=(vmem, vmem),
        scratch_shapes=[
            pltpu.VMEM((2, 32, 32, 128), F32),
            pltpu.VMEM((SHELLS * 32, HALF * 32), BF16),
            pltpu.VMEM((HALF * 32, 640), BF16),
            pltpu.VMEM((2, 2 * HALF, 32, 384), F32),
            pltpu.VMEM((2, HALF, 64, 512), BF16),
            pltpu.VMEM((2, HALF, 64, 512), BF16),
            pltpu.VMEM((HALF, 64, 512), F32),
            pltpu.VMEM((HALF, 32, 1536), BF16),
            pltpu.VMEM((HALF, 32, 1536), BF16),
            pltpu.VMEM((HALF, 32, 512), F32),
            pltpu.VMEM((2 * HALF, 32, 384), F32),
        ],
        compiler_params=pltpu.CompilerParams(vmem_limit_bytes=44 * 1024 * 1024),
    )(*args)


def remote(src, dst, send, recv, device):
    return pltpu.make_async_remote_copy(
        src_ref=src, dst_ref=dst, send_sem=send, recv_sem=recv,
        device_id=device, device_id_type=pl.DeviceIdType.MESH,
    )


def gather_kernel(
    G, N, even, odd, main, packed, stage, pack,
    send_a, recv_a, send_b, recv_b, send_h, recv_h, send_c, recv_c, send_d, recv_d,
):
    slots = 32 // N
    per = G // N
    g, s = lax.axis_index("gy"), lax.axis_index("gx")
    barrier = pltpu.get_barrier_semaphore()
    for i in range(1, G):
        pl.semaphore_signal(
            barrier, inc=1, device_id=(lax.rem(g + i, G), s), device_id_type=pl.DeviceIdType.MESH
        )
    for i in range(1, N):
        pl.semaphore_signal(
            barrier, inc=1, device_id=(g, lax.rem(s + i, N)), device_id_type=pl.DeviceIdType.MESH
        )
    pl.semaphore_wait(barrier, G + N - 2)

    def rows_of(k):
        return pl.ds(pl.multiple_of(16 * k, 16), 16)

    def copy_a(i, h):
        to = lax.rem(g + i, G)
        src = (even, odd)[h]
        return remote(
            src.at[:, rows_of(to), :], stage.at[i, h], send_a.at[i, h], recv_a.at[i, h], (to, s)
        )

    for i in range(1, G):
        for h in range(2):
            copy_a(i, h).start()
    stage[0, 0] = even[:, rows_of(g), :]
    stage[0, 1] = odd[:, rows_of(g), :]

    def source(i):
        g0 = lax.rem(g + G - i, G)
        return g0 // per, lax.rem(g0, per)

    def part(t, z, r):
        return main.at[t, :, pl.ds(slots * z, slots), pl.ds(r, 16), :]

    def copy_b(i):
        c, t = source(i)
        return remote(stage.at[i], part(t, s, 0), send_b.at[i], recv_b.at[s, t], (g, c))

    def local_b(i):
        t = source(i)[1]
        return pltpu.make_async_copy(stage.at[i], part(t, s, 0), send_b.at[i])

    def copy_h(i):
        c = source(i)[0] - 1
        return remote(
            pack.at[i], packed.at[s, :, pl.ds(0, 16), :], send_h.at[i], recv_h.at[s], (g, c)
        )

    for i in range(G):
        if i:
            for h in range(2):
                copy_a(i, h).wait_recv()
        c, t = source(i)

        @pl.when(c == s)
        def _():
            local_b(i).start()

        @pl.when(c != s)
        def _():
            copy_b(i).start()

        @pl.when((t == 0) & (c > 0))
        def _():
            for h in range(2):
                pack[i, h] = sum(place_lanes(stage[i, h, k], k) for k in range(slots))

        @pl.when((t == 0) & (c > 0) & (c != s + 1))
        def _():
            copy_h(i).start()

        @pl.when((t == 0) & (c > 0) & (c == s + 1))
        def _():
            packed[s, :, 0:16, :] = pack[i]

    for i in range(G):

        @pl.when(source(i)[0] == s)
        def _():
            local_b(i).wait()

    def copy_c(j, t):
        z = lax.rem(s + j, N)
        return remote(part(t, z, 0), part(t, z, 16), send_c.at[j, t], recv_c.at[j, t], (g - 1, s))

    def wait_b(j, t):
        z = lax.rem(s + j, N)
        remote(part(t, z, 0), part(t, z, 0), send_c.at[j, t], recv_b.at[z, t], (g, z)).wait_recv()

    order = [0] + [k for d in range(1, N) for k in (d, N - d)]
    order = list(dict.fromkeys(order))
    for j in order:
        for t in range(per):
            if j:
                wait_b(j, t)

            @pl.when(g > 0)
            def _():
                copy_c(j, t).start()

    @pl.when(s < N - 1)
    def _():
        for j in range(1, N):
            z = lax.rem(s + j, N)
            block = packed.at[z, :, pl.ds(0, 16), :]
            remote(block, block, send_d.at[0], recv_h.at[z], (g, z)).wait_recv()

    @pl.when(s == N - 1)
    def _():
        packed[:, :, 0:16, :] = jnp.zeros((N, 2, 16, 128), F32)

    def copy_d():
        return remote(
            packed.at[:, :, pl.ds(0, 16), :], packed.at[:, :, pl.ds(16, 16), :],
            send_d.at[0], recv_d.at[0], (g - 1, s),
        )

    @pl.when(g > 0)
    def _():
        copy_d().start()

    @pl.when(g == G - 1)
    def _():
        packed[:, :, 16:32, :] = jnp.zeros((N, 2, 16, 128), F32)
        main[:, :, :, 16:32, :] = jnp.zeros((per, 2, 32, 16, 128), F32)

    @pl.when(g < G - 1)
    def _():
        for j in order:
            for t in range(per):
                copy_c(j, t).wait_recv()
        copy_d().wait_recv()

    for i in range(1, G):
        for h in range(2):
            copy_a(i, h).wait_send()
    for i in range(G):
        c, t = source(i)

        @pl.when(c != s)
        def _():
            copy_b(i).wait_send()

        @pl.when((t == 0) & (c > 0) & (c != s + 1))
        def _():
            copy_h(i).wait_send()

    @pl.when(g > 0)
    def _():
        for j in order:
            for t in range(per):
                copy_c(j, t).wait_send()
        copy_d().wait_send()


def gather(even, odd):
    G, N = lax.axis_size("gy"), lax.axis_size("gx")
    slots, per = 32 // N, G // N
    vmem = pl.BlockSpec(memory_space=pltpu.VMEM)
    dma = pltpu.SemaphoreType.DMA
    return pl.pallas_call(
        functools.partial(gather_kernel, G, N),
        out_shape=(
            jax.ShapeDtypeStruct((per, 2, 32, 32, 128), F32),
            jax.ShapeDtypeStruct((N, 2, 32, 128), F32),
        ),
        in_specs=[vmem, vmem],
        out_specs=(vmem, vmem),
        scratch_shapes=[
            pltpu.VMEM((G, 2, slots, 16, 128), F32),
            pltpu.VMEM((G, 2, 16, 128), F32),
            dma((G, 2)), dma((G, 2)), dma((G,)), dma((N, per)), dma((G,)), dma((N,)),
            dma((N, per)), dma((N, per)), dma((1,)), dma((1,)),
        ],
        compiler_params=pltpu.CompilerParams(
            collective_id=0, has_side_effects=True, vmem_limit_bytes=12 * 1024 * 1024
        ),
    )(even, odd)


def spill_kernel(G, N, body, tail, out, rows, top, low, send, recv):
    g, s = lax.axis_index("gy"), lax.axis_index("gx")
    barrier = pltpu.get_barrier_semaphore()
    steps = ((1, 0), (0, 1), (1, 1))

    def ahead(dg, ds):
        return (g < G - dg) & (s < N - ds)

    def behind(dg, ds):
        return (g >= dg) & (s >= ds)

    for dg, ds in steps:

        @pl.when(ahead(dg, ds))
        def _():
            pl.semaphore_signal(
                barrier, inc=1, device_id=(g + dg, s + ds), device_id_type=pl.DeviceIdType.MESH
            )

        @pl.when(behind(dg, ds))
        def _():
            pl.semaphore_signal(
                barrier, inc=1, device_id=(g - dg, s - ds), device_id_type=pl.DeviceIdType.MESH
            )

    peers = sum(f(*d).astype(jnp.int32) for f in (ahead, behind) for d in steps)
    pl.semaphore_wait(barrier, peers)

    sources = (
        body.at[:, :, pl.ds(16, 16), :], tail.at[:, pl.ds(0, 16), :], tail.at[:, pl.ds(16, 16), :]
    )
    targets = (rows, top, low)

    def copy(k):
        dg, ds = steps[k]
        return remote(sources[k], targets[k], send.at[k], recv.at[k], (g + dg, s + ds))

    for k in range(3):

        @pl.when(ahead(*steps[k]))
        def _():
            copy(k).start()

        @pl.when(jnp.logical_not(behind(*steps[k])))
        def _():
            targets[k][...] = jnp.zeros(targets[k].shape, F32)

    for k in range(3):

        @pl.when(behind(*steps[k]))
        def _():
            copy(k).wait_recv()

    for z in range(32):
        q = z // 8
        rim = head_lanes(top[q] + low[q], z % 8)
        out[z, :, :128] = body[0, z, :16, :] + rows[0, z] + rim
        out[z, :, 128:] = body[1, z, :16, :] + rows[1, z]
    for k in range(3):

        @pl.when(ahead(*steps[k]))
        def _():
            copy(k).wait_send()


def spill(body, tail):
    G, N = lax.axis_size("gy"), lax.axis_size("gx")
    vmem = pl.BlockSpec(memory_space=pltpu.VMEM)
    dma = pltpu.SemaphoreType.DMA
    return pl.pallas_call(
        functools.partial(spill_kernel, G, N),
        out_shape=jax.ShapeDtypeStruct((32, 16, 256), F32),
        in_specs=[vmem, vmem],
        out_specs=vmem,
        scratch_shapes=[
            pltpu.VMEM((2, 32, 16, 128), F32),
            pltpu.VMEM((4, 16, 128), F32),
            pltpu.VMEM((4, 16, 128), F32),
            dma((3,)), dma((3,)),
        ],
        compiler_params=pltpu.CompilerParams(
            collective_id=1, has_side_effects=True, vmem_limit_bytes=12 * 1024 * 1024
        ),
    )(body, tail)


def on_device(even_half, odd_half, slab_slices, shells):
    main, packed = gather(even_half, odd_half)
    body, tail = filter_tile(main, packed, slab_slices, shells)
    return spill(body, tail)


def solution(mesh):
    in_specs = (P("gx", None, "gy"), P("gx", None, "gy"), P(), P())
    out_specs = P(None, "gy", "gx")
    return jax.shard_map(
        on_device, mesh=mesh, in_specs=in_specs, out_specs=out_specs, check_vma=False
    )
```
